32 devices in a mesh: wide: 8 (over z, core), narrow: 4 (over y, x).
Axes of the slice: x: 2, y: 2, z: 4, core: 2. Of those that a mesh axis runs over, the one named last changes fastest.
Arguments:
- features: float32 [12288, 512], P(('wide', 'narrow')), may hold values from -6 to 6
- weight: float32 [512, 512], replicated, may hold values from -0.25 to 0.25
- bias_vec: float32 [512], replicated, may hold values from -3 to 3
- adj_tiles: float32 [96, 8, 2, 128, 128], P('narrow', 'wide'), may hold values from -0.125 to 0.125
- pattern: int32 [96, 8, 2], P('narrow', 'wide'), may hold values from 0 to 11, as said below
- upstream: float32 [12288, 512], P(('narrow', 'wide')), may hold values from -6 to 6
Outputs:
- output: float32 [12288, 512], P(('narrow', 'wide'))
- input_grad: float32 [12288, 512], P(('wide', 'narrow'))
- weight_grad: float32 [512, 512], replicated
- bias_grad: float32 [512], replicated
The draws below stay inside these ranges and needn't reach their ends.
Inputs may be any that keep to these rules, and one draw needn't show every extreme that they name: Within one block row and group the 2 entries differ; tile t of block row r in group g lies in block column g * 12 + pattern[r, g, t].
All inputs are finite; a program needn't handle non-finite values.
Results may differ from the reference program's by a relative error of at most 0.0003.
Values sent between devices are 32-bit elements; how exact they have to be, the bound alone decides.
No kernel may reach another device: no remote copies, remote signals or barrier semaphores. Data moves between devices by JAX's collectives and lax.ppermute only.
A program may use at most 64 MiB of HBM per device.

```python
import math
import jax
import jax.numpy as jnp
from jax import lax

D = 512
BS = 128
TPB = 16
NBR = 96
GROUPS = 8
TPW = 2
GB = 12
NODES = 12288


def draw_pattern(key, part):
    scores = jax.random.randint(key, (NBR, GROUPS, GB), 0, 1 << 19)
    scores = scores * GB + jnp.arange(GB, dtype=jnp.int32)
    order = jnp.argsort(scores, axis=-1, stable=True)
    return order[:, :, :TPW].astype(jnp.int32)


def steps_of(rng, shape, pieces, low, high):
    loudness = 1.0
    for position, parts in pieces:
        draws = jax.random.uniform(jax.random.fold_in(jax.random.fold_in(rng, 6), position), (parts,), jnp.float32, low / len(pieces), high / len(pieces))
        loudness = loudness * jnp.repeat(jnp.exp(draws), shape[position] // parts).reshape((-1,) + (1,) * (len(shape) - 1 - position))
    return loudness


def normal_values(key, extent, spread, bound, shards=(), kind=jnp.bfloat16):
    factor_of = steps_of(key, extent, shards, -0.22, 0.18) if shards else 1.0
    drawn = jax.random.normal(key, extent, jnp.float32) * spread * factor_of
    return jnp.minimum(jnp.maximum(drawn, -bound), bound).astype(kind)


def setup_inputs(seed: int = 0) -> dict:
    arg_keys = jax.random.split(jax.random.key(seed), 7)
    return {
        "features": normal_values(arg_keys[0], (NODES, D), 1.0, 6.0, ((0, 32),), jnp.float32),
        "weight": normal_values(arg_keys[1], (D, D), D ** -0.5, 0.25, (), jnp.float32),
        "bias_vec": normal_values(arg_keys[2], (D,), 0.5, 3.0, (), jnp.float32),
        "adj_tiles": normal_values(arg_keys[3], (NBR, GROUPS, TPW, BS, BS), (TPB * BS) ** -0.5, 0.125, ((0, 4), (1, 8)), jnp.float32),
        "pattern": draw_pattern(jax.random.fold_in(arg_keys[6], 71), 0),
        "upstream": normal_values(arg_keys[5], (NODES, D), 1.0, 6.0, ((0, 32),), jnp.float32),
    }


highest = lax.Precision.HIGHEST

def reference(features, weight, bias_vec, adj_tiles, pattern, upstream):
    projected = jnp.dot(features, weight, precision=highest, preferred_element_type=jnp.float32)
    blocks = projected.reshape(NBR, BS, D)
    offsets = (jnp.arange(GROUPS, dtype=jnp.int32) * GB)[:, None]

    def forward_row(row_item):
        tile_row, col_ids = row_item
        block_index = (offsets + col_ids).reshape(-1).astype(jnp.int32)
        chosen = blocks[block_index].reshape(GROUPS, TPW, BS, D)
        return jnp.einsum('gtij,gtjd->id', tile_row, chosen, precision=highest)
    aggregated = lax.map(forward_row, (adj_tiles, pattern)).reshape(NODES, D)
    preact = aggregated + bias_vec
    sigmoid_z = jax.nn.sigmoid(preact)
    output = preact * sigmoid_z
    grads = upstream * sigmoid_z * (1.0 + preact * (1.0 - sigmoid_z))
    grad_blocks = grads.reshape(NBR, BS, D)

    def backward_row(running, row_item):
        tile_row, col_ids, grad_row = row_item
        block_index = (offsets + col_ids).reshape(-1).astype(jnp.int32)
        contrib = jnp.einsum('gtij,id->gtjd', tile_row, grad_row, precision=highest).reshape(GROUPS * TPW, BS, D)
        return (running.at[block_index].add(contrib), None)
    zero_grad = jnp.zeros((NBR, BS, D), jnp.float32)
    column_grad, _ = lax.scan(backward_row, zero_grad, (adj_tiles, pattern, grad_blocks))
    column_grad = column_grad.reshape(NODES, D)
    input_grad = lax.dot_general(column_grad, weight, (((1,), (1,)), ((), ())), precision=highest)
    grad_scale = 1.0 / math.sqrt(NODES)
    weight_grad = lax.dot_general(features, column_grad, (((0,), (0,)), ((), ())), precision=highest) * grad_scale
    bias_grad = lax.optimization_barrier(jnp.sum(grads, axis=0)) * grad_scale
    return (output, input_grad, weight_grad, bias_grad)
```

```python
import functools
import math

import jax
import jax.numpy as jnp
from jax import lax
from jax.experimental import pallas as pl
from jax.experimental.pallas import tpu as pltpu
from jax.sharding import PartitionSpec as P

F32 = jnp.float32
BF16 = jnp.bfloat16
HIGH = lax.Precision.HIGH
WIDTHS = (1, 1, 1, 1)
EARLY = 3
WAVES = (False, False, True)
ORDER = ('01201p2x0101x02120x3123013203023101232v3v123v123wvwwvw3wv0bw', 'vbwv3wbvw')
SMALL_VMEM = 12 * 1024 * 1024
VMEM_LIMIT = 40 * 1024 * 1024
STAGE = 16000000000.0


def cost(stages=1.0):
    return pl.CostEstimate(flops=int(STAGE * stages), bytes_accessed=0, transcendentals=0)


def split(x):
    hi = x.astype(BF16)
    return hi, (x - hi.astype(F32)).astype(BF16)


def mm(a, b):
    return jnp.dot(a, b, preferred_element_type=F32)


def bits_of(size):
    return [1 << k for k in range(size.bit_length() - 1)]


def swap(x, dim):
    axis, bit = dim
    size = lax.axis_size(axis)
    return lax.ppermute(x, axis, [(i, i ^ bit) for i in range(size)])


ROWS = 64


def rows_call(fn, out_rows, xs, extra=()):
    width = xs[0].shape[1]
    outs = [jax.ShapeDtypeStruct((rows, width), F32) for rows in out_rows]
    count, every = len(xs), len(xs) + len(extra)

    def kernel(*refs):
        fn(refs[:count], refs[count:every], refs[every:])

    vmem = pl.BlockSpec(memory_space=pltpu.VMEM)
    return pl.pallas_call(
        kernel,
        in_specs=[vmem] * every,
        out_specs=[vmem] * len(outs),
        out_shape=outs,
        compiler_params=pltpu.CompilerParams(vmem_limit_bytes=SMALL_VMEM),
        cost_estimate=cost(),
    )(*xs, *extra)


def blocks_of(rows, step):
    unit = math.gcd(rows, ROWS)

    @pl.loop(0, rows // unit)
    def _(k):
        step(pl.multiple_of(k * unit, unit), unit)


def add_halves(keep, got):
    half = keep.shape[0] // 2

    def fn(ins, _, outs):
        for k, out in enumerate(outs):

            def step(at, unit, k=k, out=out):
                rows = pl.ds(k * half + at, unit)
                out[pl.ds(at, unit), :] = ins[0][rows, :] + ins[1][rows, :]

            blocks_of(half, step)

    return rows_call(fn, [half, half], [keep, got])


def stack(parts):
    def fn(ins, _, outs):
        base = 0
        for ref in ins:

            def step(at, unit, base=base, ref=ref):
                outs[0][pl.ds(base + at, unit), :] = ref[pl.ds(at, unit), :]

            blocks_of(ref.shape[0], step)
            base += ref.shape[0]

    return rows_call(fn, [sum(p.shape[0] for p in parts)], parts)[0]


def add_all(terms):
    def fn(ins, _, outs):
        def step(at, unit):
            rows = pl.ds(at, unit)
            total = ins[0][rows, :]
            for ref in ins[1:]:
                total = total + ref[rows, :]
            outs[0][rows, :] = total

        blocks_of(outs[0].shape[0], step)

    return rows_call(fn, [terms[0].shape[0]], terms)[0]


def activate(keep, got, upstream, bias):
    def fn(ins, extra, outs):
        def step(at, unit):
            rows = pl.ds(at, unit)
            preact = ins[0][rows, :] + ins[1][rows, :] + extra[0][...]
            gate = jax.nn.sigmoid(preact)
            outs[0][rows, :] = preact * gate
            outs[1][rows, :] = ins[2][rows, :] * gate * (1.0 + preact * (1.0 - gate))

        blocks_of(outs[0].shape[0], step)

    rows = keep.shape[0]
    return rows_call(fn, [rows, rows], [keep, got, upstream], [bias.reshape(1, -1)])


class Line:
    def __init__(self):
        self.last = None

    def enter(self, xs):
        if self.last is not None:
            xs, self.last = lax.optimization_barrier((xs, self.last))
        return xs

    def leave(self, xs):
        self.last = xs
        return xs


def gather_stages(line, x, dims, out, waves):
    parts = [x]
    if waves and len(dims) == 2:
        first, second = swap(x, dims[0]), swap(x, dims[1])
        yield
        last = swap(line.leave(stack([line.enter(first)])), dims[1])
        parts = [x, first, second, last]
    else:
        for dim in dims:
            if len(parts) > 1:
                yield
                parts = line.enter(parts)
                parts = [line.leave(stack(parts))]
            parts = parts + [swap(parts[0], dim)]
    yield
    out.extend(line.enter(parts))


def halve_stages(line, keep, send, dims, out):
    for k, dim in enumerate(dims):
        got = swap(send, dim)
        yield
        keep, got = line.enter((keep, got))
        if k + 1 == len(dims):
            out.extend((keep, got))
        else:
            keep, send = line.leave(add_halves(keep, got))


def slot_of(owner, me, labels):
    s = owner ^ me
    last = len(labels) - 1
    return sum(((s // label) & 1) << (last - k) for k, label in enumerate(labels))


def slot_order(labels):
    order = [0]
    for label in reversed(labels):
        order = order + [s ^ label for s in order]
    return order


def prep_kernel(tiles_ref, hi_ref, lo_ref, hit_ref, lot_ref):
    steps, per_group, size, _ = tiles_ref.shape
    for r in range(steps):
        for t in range(per_group):
            tile = tiles_ref[r, t]
            hi, lo = split(tile)
            cols = pl.ds(t * size, size)
            hi_ref[r, :, cols] = hi
            lo_ref[r, :, cols] = lo
            hi, lo = split(tile.T)
            hit_ref[r, cols, :] = hi
            lot_ref[r, cols, :] = lo


def prep(tiles, step):
    rows, per_group, size, _ = tiles.shape
    wide = jax.ShapeDtypeStruct((rows, size, per_group * size), BF16)
    tall = jax.ShapeDtypeStruct((rows, per_group * size, size), BF16)
    return pl.pallas_call(
        prep_kernel,
        grid=(rows // step,),
        in_specs=[pl.BlockSpec((step, per_group, size, size), lambda i: (i, 0, 0, 0))],
        out_specs=[pl.BlockSpec((step,) + s.shape[1:], lambda i: (i, 0, 0)) for s in (wide, wide, tall, tall)],
        out_shape=[wide, wide, tall, tall],
        compiler_params=pltpu.CompilerParams(vmem_limit_bytes=VMEM_LIMIT),
        cost_estimate=cost(0),
    )(tiles)


def load_split(refs, hi, lo):
    base = 0
    for ref in refs:
        rows = ref.shape[0]
        hi[pl.ds(base, rows), :], lo[pl.ds(base, rows), :] = split(ref[...])
        base += rows


def block_rows_at(start, size, unit, own_rows, place):
    at = []
    for q in range(size // unit):
        row = start + q * unit
        w = place(row // own_rows) * own_rows + row % own_rows
        at.append(pl.multiple_of(w, unit))
    return at


def products(a_hi, a_lo, b_hi, b_lo):
    return mm(a_hi, b_hi) + (mm(a_hi, b_lo) + mm(a_lo, b_hi))


def gathered(ref, at, unit):
    return jnp.concatenate([ref[pl.ds(w, unit), :] for w in at], axis=0) if len(at) > 1 else ref[pl.ds(at[0], unit), :]


def forward_kernel(own_rows, wide_labels, narrow_labels, me, pattern, a_hi, a_lo, *rest):
    *p_refs, keep, send, p_hi, p_lo, total = rest
    step = pl.program_id(0)
    rows, size, depth = a_hi.shape
    per_group = depth // size
    unit = math.gcd(own_rows, size)

    @pl.when(step == 0)
    def _():
        load_split(p_refs, p_hi, p_lo)

    for i in range(rows):
        r = step * rows + i
        at = []
        for t in range(per_group):
            start = pattern[r * per_group + t] * size
            at += block_rows_at(start, size, unit, own_rows, lambda o: slot_of(o, me[1], narrow_labels))
        acc = products(a_hi[i], a_lo[i], gathered(p_hi, at, unit), gathered(p_lo, at, unit))
        out_at = block_rows_at(r * size, size, unit, own_rows, lambda o: slot_of(o, me[0], wide_labels))
        for q, w in enumerate(out_at):
            total[pl.ds(w, unit), :] = acc[q * unit : (q + 1) * unit]

    @pl.when(step == pl.num_programs(0) - 1)
    def _():
        half = keep.shape[0]
        keep[...] = total[:half]
        send[...] = total[half:]


def tile_call(kernel, me, pattern, a_hi, a_lo, slots, step, outs, total_rows):
    rows = a_hi.shape[0]
    width = slots[0].shape[1]
    in_rows = sum(s.shape[0] for s in slots)
    whole = lambda s: pl.BlockSpec(s, lambda i, *_: (0, 0))
    tile = pl.BlockSpec((step,) + a_hi.shape[1:], lambda i, *_: (i, 0, 0))
    outs = [jax.ShapeDtypeStruct((n, width), F32) for n in outs]
    return pl.pallas_call(
        kernel,
        grid_spec=pltpu.PrefetchScalarGridSpec(
            num_scalar_prefetch=2,
            grid=(rows // step,),
            in_specs=[tile, tile] + [whole(s.shape) for s in slots],
            out_specs=[whole(o.shape) for o in outs],
            scratch_shapes=[
                pltpu.VMEM((in_rows, width), BF16),
                pltpu.VMEM((in_rows, width), BF16),
                pltpu.VMEM((total_rows, width), F32),
            ],
        ),
        out_shape=outs,
        compiler_params=pltpu.CompilerParams(vmem_limit_bytes=VMEM_LIMIT),
        cost_estimate=cost(),
    )(me, pattern, a_hi, a_lo, *slots)


def backward_kernel(own_rows, wide_labels, narrow_labels, me, pattern, a_hi, a_lo, *rest):
    *g_refs, keep, send, sums, g_hi, g_lo, total = rest
    step = pl.program_id(0)
    rows, depth, size = a_hi.shape
    per_group = depth // size
    unit = math.gcd(own_rows, size)

    @pl.when(step == 0)
    def _():
        load_split(g_refs, g_hi, g_lo)
        total[...] = jnp.zeros_like(total)
        sums[...] = sum(jnp.sum(ref[...].reshape(-1, 8, ref.shape[1]), axis=0) for ref in g_refs)

    for i in range(rows):
        r = step * rows + i
        at = block_rows_at(r * size, size, unit, own_rows, lambda o: slot_of(o, me[0], wide_labels))
        acc = products(a_hi[i], a_lo[i], gathered(g_hi, at, unit), gathered(g_lo, at, unit))
        for t in range(per_group):
            start = pattern[r * per_group + t] * size
            out_at = block_rows_at(start, size, unit, own_rows, lambda o: slot_of(o, me[1], narrow_labels))
            for q, w in enumerate(out_at):
                total[pl.ds(w, unit), :] += acc[t * size + q * unit : t * size + (q + 1) * unit]

    @pl.when(step == pl.num_programs(0) - 1)
    def _():
        half = keep.shape[0]
        keep[...] = total[:half]
        send[...] = total[half:]


def turn_kernel(*refs):
    *x_refs, hi, lo = refs
    base = 0
    for ref in x_refs:
        cols = pl.ds(base, ref.shape[0])
        hi[:, cols], lo[:, cols] = split(ref[...].T)
        base += ref.shape[0]


def turn(slots):
    rows = sum(s.shape[0] for s in slots)
    out = jax.ShapeDtypeStruct((slots[0].shape[1], rows), BF16)
    return pl.pallas_call(
        turn_kernel,
        out_shape=[out, out],
        compiler_params=pltpu.CompilerParams(vmem_limit_bytes=VMEM_LIMIT),
        cost_estimate=cost(),
    )(*slots)


def outer_kernel(labels, orders, me, x_hi, x_lo, *rest):
    *s_refs, keep, send, total = rest
    feats, count = x_hi.shape
    pieces = 1 << len(labels)
    unit = feats // pieces
    base = 0
    for k, order in enumerate(orders):
        refs = s_refs[2 * k : 2 * k + 2]
        width = refs[0].shape[1]
        own = count // len(order)
        half = len(order) // 2
        acc = None
        for j, s in enumerate(order):
            cols = pl.ds(s * own, own)
            rows = refs[j // half][pl.ds((j % half) * own, own), :]
            part = products(x_hi[:, cols], x_lo[:, cols], *split(rows))
            acc = part if acc is None else acc + part
        for q in range(pieces):
            w = slot_of(q, me[2], labels) * unit
            total[pl.ds(pl.multiple_of(w, unit), unit), pl.ds(base, width)] = acc[q * unit : (q + 1) * unit]
        base += width
    half = feats // 2
    keep[...] = total[:half]
    send[...] = total[half:]


def outer(me, x_hi, x_lo, parts, labels, orders):
    feats = x_hi.shape[0]
    width = sum(s.shape[1] for s in parts) // 2
    out = jax.ShapeDtypeStruct((feats // 2, width), F32)
    vmem = pl.BlockSpec(memory_space=pltpu.VMEM)
    return pl.pallas_call(
        functools.partial(outer_kernel, labels, orders),
        in_specs=[pl.BlockSpec(memory_space=pltpu.SMEM)] + [vmem] * (2 + len(parts)),
        out_specs=[vmem, vmem],
        out_shape=[out, out],
        scratch_shapes=[pltpu.VMEM((feats, width), F32)],
        compiler_params=pltpu.CompilerParams(vmem_limit_bytes=VMEM_LIMIT),
        cost_estimate=cost(),
    )(me, x_hi, x_lo, *parts)


def place_kernel(scale, labels, me, *refs):
    *p_refs, out = refs
    order = slot_order(labels)
    unit = out.shape[0] // len(order)
    half = len(order) // 2
    for k, s in enumerate(order):
        part = p_refs[k // half][pl.ds((k % half) * unit, unit), :]
        out[pl.ds(pl.multiple_of((me[2] ^ s) * unit, unit), unit), :] = part * scale


def place(me, parts, labels, scale):
    rows, width = parts[0].shape
    vmem = pl.BlockSpec(memory_space=pltpu.VMEM)
    return pl.pallas_call(
        functools.partial(place_kernel, scale, labels),
        in_specs=[pl.BlockSpec(memory_space=pltpu.SMEM)] + [vmem] * len(parts),
        out_specs=vmem,
        out_shape=jax.ShapeDtypeStruct((rows * len(parts), width), F32),
        compiler_params=pltpu.CompilerParams(vmem_limit_bytes=VMEM_LIMIT),
        cost_estimate=cost(),
    )(me, *parts)


def body(features, weight, bias_vec, adj_tiles, pattern, upstream):
    own_rows, feat_width = features.shape
    block_rows, _, per_group, size, _ = adj_tiles.shape
    n_wide, n_narrow = lax.axis_size("wide"), lax.axis_size("narrow")
    me_wide, me_narrow = lax.axis_index("wide"), lax.axis_index("narrow")
    step = math.gcd(block_rows, 6)
    widths = [w * feat_width // sum(WIDTHS) for w in WIDTHS]
    edges = [sum(widths[:c]) for c in range(len(widths) + 1)]
    count = len(widths)
    grad_scale = 1.0 / math.sqrt(own_rows * n_wide * n_narrow)
    line = Line()

    core = ("wide", 1)
    z_bits = bits_of(n_wide)[1:]
    z_dims = [("wide", b) for b in z_bits]
    narrow_bits = bits_of(n_narrow)
    narrow_dims = [("narrow", b) for b in narrow_bits]
    wide_labels = [1] + z_bits
    sum_labels = [1] + [2 * b for b in narrow_bits]
    me = jnp.stack([me_wide, me_narrow, me_wide % 2 + 2 * me_narrow]).astype(jnp.int32)
    pattern = pattern.reshape(-1)

    tiles = []

    outputs, column_grads, halves, sums = [None] * count, [None] * count, [None] * count, [None] * count
    turned = []

    def chunk_bits(c):
        return narrow_bits if c % 2 == 0 else narrow_bits[::-1]

    def chunk(c):
        cols = slice(edges[c], edges[c + 1])
        n_bits = chunk_bits(c)
        n_dims = [("narrow", b) for b in n_bits]

        own = line.enter(features)
        own = jnp.dot(own, weight[:, cols], precision=HIGH, preferred_element_type=F32)
        inputs = []
        yield from gather_stages(line, line.leave(own), n_dims[::-1], inputs, WAVES[0])
        while not tiles:
            yield
        a_hi, a_lo, at_hi, at_lo = tiles
        kernel = functools.partial(forward_kernel, own_rows, wide_labels, n_bits)
        half = block_rows * size // 2
        keep, send = line.leave(tile_call(kernel, me, pattern, a_hi, a_lo, inputs, step, [half, half], 2 * half))
        got = swap(send, core)
        yield
        keep, got = line.enter((keep, got))
        keep, send = line.leave(add_halves(keep, got))
        found = []
        yield from halve_stages(line, keep, send, z_dims, found)
        outputs[c], grads = activate(*found, upstream[:, cols], bias_vec[cols])
        line.leave(grads)
        rows = []
        yield from gather_stages(line, grads, z_dims[::-1], rows, WAVES[1])
        rows = line.leave(stack(rows))
        got = swap(rows, core)
        yield
        inputs = line.enter([rows, got])
        kernel = functools.partial(backward_kernel, own_rows, wide_labels, n_bits)
        half = own_rows * n_narrow // 2
        keep, send, sums[c] = line.leave(
            tile_call(kernel, me, pattern, at_hi, at_lo, inputs, step, [half, half, 8], 2 * half)
        )
        halves[c] = (keep, send)
        found = []
        yield from halve_stages(line, keep, send, n_dims, found)
        column_grads[c] = line.leave(add_all(found))

    def tile_parts():
        own = line.enter(adj_tiles).reshape(block_rows, per_group, size, size)
        tiles.extend(line.leave(prep(own, step)))
        yield

    def feature_rows():
        slots = []
        yield from gather_stages(line, line.enter(features), narrow_dims[::-1], slots, WAVES[2])
        turned.extend(line.leave(turn(slots)))

    def weight_stages(first, last, out):
        while not turned or None in halves[first:last]:
            yield
        there = slot_order(narrow_bits)
        orders = [[there.index(s) for s in slot_order(chunk_bits(c))] for c in range(first, last)]
        parts = [h for c in range(first, last) for h in halves[c]]
        x_hi, x_lo, *parts = line.enter(list(turned) + parts)
        keep, send = line.leave(outer(me, x_hi, x_lo, parts, sum_labels, orders))
        found = []
        yield from halve_stages(line, keep, send, [core] + narrow_dims, found)
        total = line.leave(add_all(found))
        for dim in z_dims:
            got = swap(total, dim)
            yield
            total, got = line.enter((total, got))
            total = line.leave(add_all([total, got]))
        parts = []
        yield from gather_stages(line, total, narrow_dims[::-1], parts, False)
        parts = line.leave(stack(parts))
        got = swap(parts, core)
        yield
        out.append(line.leave(place(me, line.enter([parts, got]), sum_labels, grad_scale)))

    def bias_stages(out):
        while None in halves:
            yield
        total = line.leave(jnp.concatenate(sums, axis=1))
        for dim in narrow_dims:
            got = swap(total, dim)
            yield
            total, got = line.enter((total, got))
            total = line.leave(total + got)
        out.append(jnp.sum(total, axis=0) * grad_scale)

    early_parts, weight_parts, bias_out = [], [], []
    lines = {"p": tile_parts()}
    lines.update({str(c): chunk(c) for c in range(count)})
    lines["x"] = feature_rows()
    first = EARLY
    if first:
        lines["v"] = weight_stages(0, first, early_parts)
    lines["w"] = weight_stages(first, count, weight_parts)
    lines["b"] = bias_stages(bias_out)
    for k, name in enumerate("".join(ORDER)):
        with jax.named_scope(f"stage_{name}_{k}"):
            next(lines[name] if name in lines else iter(()), None)
    for stages in lines.values():
        for _ in stages:
            pass
    column_grad = jnp.concatenate(column_grads, axis=1)
    input_grad = lax.dot_general(column_grad, weight, (((1,), (1,)), ((), ())), precision=HIGH)
    return (
        jnp.concatenate(outputs, axis=1),
        input_grad,
        jnp.concatenate(early_parts + weight_parts, axis=1),
        bias_out[0],
    )


def solution(mesh):
    in_specs = (
        P(("wide", "narrow"), None),
        P(),
        P(),
        P("narrow", "wide", None, None, None),
        P("narrow", "wide", None),
        P(("narrow", "wide"), None),
    )
    out_specs = (P(("narrow", "wide"), None), P(("wide", "narrow"), None), P(), P())
    return jax.shard_map(body, mesh=mesh, in_specs=in_specs, out_specs=out_specs, check_vma=False)
```

```python
import functools
import math

import jax
import jax.numpy as jnp
from jax import lax
from jax.experimental import pallas as pl
from jax.experimental.pallas import tpu as pltpu
from jax.sharding import PartitionSpec as P

F32 = jnp.float32
BF16 = jnp.bfloat16
HIGH = lax.Precision.HIGH
WIDTHS = (1, 1, 1, 1)
EARLY = 2
WAVES = (False, False, False)
ORDER = ('01201p32010132x021303x123120131x20302v230v30wvw21wv3wv2wvbwv', 'wbvw3vb1w')
SMALL_VMEM = 12 * 1024 * 1024
VMEM_LIMIT = 40 * 1024 * 1024
STAGE = 16000000000.0
TAIL = 0.3


def cost(stages=1.0):
    return pl.CostEstimate(flops=int(STAGE * stages), bytes_accessed=0, transcendentals=0)


def split(x):
    hi = x.astype(BF16)
    return hi, (x - hi.astype(F32)).astype(BF16)


def mm(a, b):
    return jnp.dot(a, b, preferred_element_type=F32)


def bits_of(size):
    return [1 << k for k in range(size.bit_length() - 1)]


def swap(x, dim):
    axis, bit = dim
    size = lax.axis_size(axis)
    return lax.ppermute(x, axis, [(i, i ^ bit) for i in range(size)])


ROWS = 64


def rows_call(fn, out_rows, xs, extra=(), stages=1.0):
    width = xs[0].shape[1]
    outs = [jax.ShapeDtypeStruct((rows, width), F32) for rows in out_rows]
    count, every = len(xs), len(xs) + len(extra)

    def kernel(*refs):
        fn(refs[:count], refs[count:every], refs[every:])

    vmem = pl.BlockSpec(memory_space=pltpu.VMEM)
    return pl.pallas_call(
        kernel,
        in_specs=[vmem] * every,
        out_specs=[vmem] * len(outs),
        out_shape=outs,
        compiler_params=pltpu.CompilerParams(vmem_limit_bytes=SMALL_VMEM),
        cost_estimate=cost(stages),
    )(*xs, *extra)


def blocks_of(rows, step):
    unit = math.gcd(rows, ROWS)

    @pl.loop(0, rows // unit)
    def _(k):
        step(pl.multiple_of(k * unit, unit), unit)


def add_halves(keep, got, stages=1.0):
    half = keep.shape[0] // 2

    def fn(ins, _, outs):
        for k, out in enumerate(outs):

            def step(at, unit, k=k, out=out):
                rows = pl.ds(k * half + at, unit)
                out[pl.ds(at, unit), :] = ins[0][rows, :] + ins[1][rows, :]

            blocks_of(half, step)

    return rows_call(fn, [half, half], [keep, got], stages=stages)


def stack(parts, stages=1.0):
    def fn(ins, _, outs):
        base = 0
        for ref in ins:

            def step(at, unit, base=base, ref=ref):
                outs[0][pl.ds(base + at, unit), :] = ref[pl.ds(at, unit), :]

            blocks_of(ref.shape[0], step)
            base += ref.shape[0]

    return rows_call(fn, [sum(p.shape[0] for p in parts)], parts, stages=stages)[0]


def add_all(terms, stages=1.0):
    def fn(ins, _, outs):
        def step(at, unit):
            rows = pl.ds(at, unit)
            total = ins[0][rows, :]
            for ref in ins[1:]:
                total = total + ref[rows, :]
            outs[0][rows, :] = total

        blocks_of(outs[0].shape[0], step)

    return rows_call(fn, [terms[0].shape[0]], terms, stages=stages)[0]


def activate(keep, got, upstream, bias):
    def fn(ins, extra, outs):
        def step(at, unit):
            rows = pl.ds(at, unit)
            preact = ins[0][rows, :] + ins[1][rows, :] + extra[0][...]
            gate = jax.nn.sigmoid(preact)
            outs[0][rows, :] = preact * gate
            outs[1][rows, :] = ins[2][rows, :] * gate * (1.0 + preact * (1.0 - gate))

        blocks_of(outs[0].shape[0], step)

    rows = keep.shape[0]
    return rows_call(fn, [rows, rows], [keep, got, upstream], [bias.reshape(1, -1)])


class Line:
    def __init__(self):
        self.last = None

    def enter(self, xs):
        if self.last is not None:
            xs, self.last = lax.optimization_barrier((xs, self.last))
        return xs

    def leave(self, xs):
        self.last = xs
        return xs


def gather_stages(line, x, dims, out, waves, stages=1.0):
    parts = [x]
    if waves and len(dims) == 2:
        first, second = swap(x, dims[0]), swap(x, dims[1])
        yield
        last = swap(line.leave(stack([line.enter(first)])), dims[1])
        parts = [x, first, second, last]
    else:
        for dim in dims:
            if len(parts) > 1:
                yield
                parts = line.enter(parts)
                parts = [line.leave(stack(parts, stages))]
            parts = parts + [swap(parts[0], dim)]
    yield
    out.extend(line.enter(parts))


def halve_stages(line, keep, send, dims, out, stages=1.0):
    for k, dim in enumerate(dims):
        got = swap(send, dim)
        yield
        keep, got = line.enter((keep, got))
        if k + 1 == len(dims):
            out.extend((keep, got))
        else:
            keep, send = line.leave(add_halves(keep, got, stages))


def slot_of(owner, me, labels):
    s = owner ^ me
    last = len(labels) - 1
    return sum(((s // label) & 1) << (last - k) for k, label in enumerate(labels))


def slot_order(labels):
    order = [0]
    for label in reversed(labels):
        order = order + [s ^ label for s in order]
    return order


def prep_kernel(tiles_ref, hi_ref, lo_ref, hit_ref, lot_ref):
    steps, per_group, size, _ = tiles_ref.shape
    for r in range(steps):
        for t in range(per_group):
            tile = tiles_ref[r, t]
            hi, lo = split(tile)
            cols = pl.ds(t * size, size)
            hi_ref[r, :, cols] = hi
            lo_ref[r, :, cols] = lo
            hi, lo = split(tile.T)
            hit_ref[r, cols, :] = hi
            lot_ref[r, cols, :] = lo


def prep(tiles, step):
    rows, per_group, size, _ = tiles.shape
    wide = jax.ShapeDtypeStruct((rows, size, per_group * size), BF16)
    tall = jax.ShapeDtypeStruct((rows, per_group * size, size), BF16)
    return pl.pallas_call(
        prep_kernel,
        grid=(rows // step,),
        in_specs=[pl.BlockSpec((step, per_group, size, size), lambda i: (i, 0, 0, 0))],
        out_specs=[pl.BlockSpec((step,) + s.shape[1:], lambda i: (i, 0, 0)) for s in (wide, wide, tall, tall)],
        out_shape=[wide, wide, tall, tall],
        compiler_params=pltpu.CompilerParams(vmem_limit_bytes=VMEM_LIMIT),
        cost_estimate=cost(0),
    )(tiles)


def load_split(refs, hi, lo):
    base = 0
    for ref in refs:
        rows = ref.shape[0]
        hi[pl.ds(base, rows), :], lo[pl.ds(base, rows), :] = split(ref[...])
        base += rows


def block_rows_at(start, size, unit, own_rows, place):
    at = []
    for q in range(size // unit):
        row = start + q * unit
        w = place(row // own_rows) * own_rows + row % own_rows
        at.append(pl.multiple_of(w, unit))
    return at


def products(a_hi, a_lo, b_hi, b_lo):
    return mm(a_hi, b_hi) + (mm(a_hi, b_lo) + mm(a_lo, b_hi))


def gathered(ref, at, unit):
    return jnp.concatenate([ref[pl.ds(w, unit), :] for w in at], axis=0) if len(at) > 1 else ref[pl.ds(at[0], unit), :]


def forward_kernel(own_rows, wide_labels, narrow_labels, me, pattern, a_hi, a_lo, *rest):
    *p_refs, keep, send, p_hi, p_lo, total = rest
    step = pl.program_id(0)
    rows, size, depth = a_hi.shape
    per_group = depth // size
    unit = math.gcd(own_rows, size)

    @pl.when(step == 0)
    def _():
        load_split(p_refs, p_hi, p_lo)

    for i in range(rows):
        r = step * rows + i
        at = []
        for t in range(per_group):
            start = pattern[r * per_group + t] * size
            at += block_rows_at(start, size, unit, own_rows, lambda o: slot_of(o, me[1], narrow_labels))
        acc = products(a_hi[i], a_lo[i], gathered(p_hi, at, unit), gathered(p_lo, at, unit))
        out_at = block_rows_at(r * size, size, unit, own_rows, lambda o: slot_of(o, me[0], wide_labels))
        for q, w in enumerate(out_at):
            total[pl.ds(w, unit), :] = acc[q * unit : (q + 1) * unit]

    @pl.when(step == pl.num_programs(0) - 1)
    def _():
        half = keep.shape[0]
        keep[...] = total[:half]
        send[...] = total[half:]


def tile_call(kernel, me, pattern, a_hi, a_lo, slots, step, outs, total_rows):
    rows = a_hi.shape[0]
    width = slots[0].shape[1]
    in_rows = sum(s.shape[0] for s in slots)
    whole = lambda s: pl.BlockSpec(s, lambda i, *_: (0, 0))
    tile = pl.BlockSpec((step,) + a_hi.shape[1:], lambda i, *_: (i, 0, 0))
    outs = [jax.ShapeDtypeStruct((n, width), F32) for n in outs]
    return pl.pallas_call(
        kernel,
        grid_spec=pltpu.PrefetchScalarGridSpec(
            num_scalar_prefetch=2,
            grid=(rows // step,),
            in_specs=[tile, tile] + [whole(s.shape) for s in slots],
            out_specs=[whole(o.shape) for o in outs],
            scratch_shapes=[
                pltpu.VMEM((in_rows, width), BF16),
                pltpu.VMEM((in_rows, width), BF16),
                pltpu.VMEM((total_rows, width), F32),
            ],
        ),
        out_shape=outs,
        compiler_params=pltpu.CompilerParams(vmem_limit_bytes=VMEM_LIMIT),
        cost_estimate=cost(),
    )(me, pattern, a_hi, a_lo, *slots)


def backward_kernel(own_rows, wide_labels, narrow_labels, me, pattern, a_hi, a_lo, *rest):
    *g_refs, keep, send, sums, g_hi, g_lo, total = rest
    step = pl.program_id(0)
    rows, depth, size = a_hi.shape
    per_group = depth // size
    unit = math.gcd(own_rows, size)

    @pl.when(step == 0)
    def _():
        load_split(g_refs, g_hi, g_lo)
        total[...] = jnp.zeros_like(total)
        sums[...] = sum(jnp.sum(ref[...].reshape(-1, 8, ref.shape[1]), axis=0) for ref in g_refs)

    for i in range(rows):
        r = step * rows + i
        at = block_rows_at(r * size, size, unit, own_rows, lambda o: slot_of(o, me[0], wide_labels))
        acc = products(a_hi[i], a_lo[i], gathered(g_hi, at, unit), gathered(g_lo, at, unit))
        for t in range(per_group):
            start = pattern[r * per_group + t] * size
            out_at = block_rows_at(start, size, unit, own_rows, lambda o: slot_of(o, me[1], narrow_labels))
            for q, w in enumerate(out_at):
                total[pl.ds(w, unit), :] += acc[t * size + q * unit : t * size + (q + 1) * unit]

    @pl.when(step == pl.num_programs(0) - 1)
    def _():
        half = keep.shape[0]
        keep[...] = total[:half]
        send[...] = total[half:]


def turn_kernel(*refs):
    *x_refs, hi, lo = refs
    base = 0
    for ref in x_refs:
        cols = pl.ds(base, ref.shape[0])
        hi[:, cols], lo[:, cols] = split(ref[...].T)
        base += ref.shape[0]


def turn(slots):
    rows = sum(s.shape[0] for s in slots)
    out = jax.ShapeDtypeStruct((slots[0].shape[1], rows), BF16)
    return pl.pallas_call(
        turn_kernel,
        out_shape=[out, out],
        compiler_params=pltpu.CompilerParams(vmem_limit_bytes=VMEM_LIMIT),
        cost_estimate=cost(),
    )(*slots)


def outer_kernel(labels, orders, me, x_hi, x_lo, *rest):
    *s_refs, keep, send, total = rest
    feats, count = x_hi.shape
    pieces = 1 << len(labels)
    unit = feats // pieces
    base = 0
    for k, order in enumerate(orders):
        refs = s_refs[2 * k : 2 * k + 2]
        width = refs[0].shape[1]
        own = count // len(order)
        half = len(order) // 2
        acc = None
        for j, s in enumerate(order):
            cols = pl.ds(s * own, own)
            rows = refs[j // half][pl.ds((j % half) * own, own), :]
            part = products(x_hi[:, cols], x_lo[:, cols], *split(rows))
            acc = part if acc is None else acc + part
        for q in range(pieces):
            w = slot_of(q, me[2], labels) * unit
            total[pl.ds(pl.multiple_of(w, unit), unit), pl.ds(base, width)] = acc[q * unit : (q + 1) * unit]
        base += width
    half = feats // 2
    keep[...] = total[:half]
    send[...] = total[half:]


def outer(me, x_hi, x_lo, parts, labels, orders):
    feats = x_hi.shape[0]
    width = sum(s.shape[1] for s in parts) // 2
    out = jax.ShapeDtypeStruct((feats // 2, width), F32)
    vmem = pl.BlockSpec(memory_space=pltpu.VMEM)
    return pl.pallas_call(
        functools.partial(outer_kernel, labels, orders),
        in_specs=[pl.BlockSpec(memory_space=pltpu.SMEM)] + [vmem] * (2 + len(parts)),
        out_specs=[vmem, vmem],
        out_shape=[out, out],
        scratch_shapes=[pltpu.VMEM((feats, width), F32)],
        compiler_params=pltpu.CompilerParams(vmem_limit_bytes=VMEM_LIMIT),
        cost_estimate=cost(),
    )(me, x_hi, x_lo, *parts)


def place_kernel(scale, labels, me, *refs):
    *p_refs, out = refs
    order = slot_order(labels)
    unit = out.shape[0] // len(order)
    half = len(order) // 2
    base = 0
    for g in range(0, len(p_refs), 2):
        width = p_refs[g].shape[1]
        for k, s in enumerate(order):
            part = p_refs[g + k // half][pl.ds((k % half) * unit, unit), :]
            out[pl.ds(pl.multiple_of((me[2] ^ s) * unit, unit), unit), pl.ds(base, width)] = part * scale
        base += width


def place(me, parts, labels, scale):
    rows = 2 * parts[0].shape[0]
    vmem = pl.BlockSpec(memory_space=pltpu.VMEM)
    return pl.pallas_call(
        functools.partial(place_kernel, scale, labels),
        in_specs=[pl.BlockSpec(memory_space=pltpu.SMEM)] + [vmem] * len(parts),
        out_specs=vmem,
        out_shape=jax.ShapeDtypeStruct((rows, sum(p.shape[1] for p in parts[::2])), F32),
        compiler_params=pltpu.CompilerParams(vmem_limit_bytes=VMEM_LIMIT),
        cost_estimate=cost(),
    )(me, *parts)


def body(features, weight, bias_vec, adj_tiles, pattern, upstream):
    own_rows, feat_width = features.shape
    block_rows, _, per_group, size, _ = adj_tiles.shape
    n_wide, n_narrow = lax.axis_size("wide"), lax.axis_size("narrow")
    me_wide, me_narrow = lax.axis_index("wide"), lax.axis_index("narrow")
    step = math.gcd(block_rows, 6)
    widths = [w * feat_width // sum(WIDTHS) for w in WIDTHS]
    edges = [sum(widths[:c]) for c in range(len(widths) + 1)]
    count = len(widths)
    grad_scale = 1.0 / math.sqrt(own_rows * n_wide * n_narrow)
    line = Line()

    core = ("wide", 1)
    z_bits = bits_of(n_wide)[1:]
    z_dims = [("wide", b) for b in z_bits]
    narrow_bits = bits_of(n_narrow)
    narrow_dims = [("narrow", b) for b in narrow_bits]
    wide_labels = [1] + z_bits
    sum_labels = [1] + [2 * b for b in narrow_bits]
    me = jnp.stack([me_wide, me_narrow, me_wide % 2 + 2 * me_narrow]).astype(jnp.int32)
    pattern = pattern.reshape(-1)

    tiles = []

    outputs, halves, sums = [None] * count, [None] * count, [None] * count
    input_grads, turned = [], []

    def chunk_bits(c):
        return narrow_bits if c % 2 == 0 else narrow_bits[::-1]

    def chunk(c):
        cols = slice(edges[c], edges[c + 1])
        n_bits = chunk_bits(c)
        n_dims = [("narrow", b) for b in n_bits]

        own = line.enter(features)
        own = jnp.dot(own, weight[:, cols], precision=HIGH, preferred_element_type=F32)
        inputs = []
        yield from gather_stages(line, line.leave(own), n_dims[::-1], inputs, WAVES[0])
        while not tiles:
            yield
        a_hi, a_lo, at_hi, at_lo = tiles
        kernel = functools.partial(forward_kernel, own_rows, wide_labels, n_bits)
        half = block_rows * size // 2
        keep, send = line.leave(tile_call(kernel, me, pattern, a_hi, a_lo, inputs, step, [half, half], 2 * half))
        got = swap(send, core)
        yield
        keep, got = line.enter((keep, got))
        keep, send = line.leave(add_halves(keep, got))
        found = []
        yield from halve_stages(line, keep, send, z_dims, found)
        outputs[c], grads = activate(*found, upstream[:, cols], bias_vec[cols])
        line.leave(grads)
        rows = []
        yield from gather_stages(line, grads, z_dims[::-1], rows, WAVES[1])
        rows = line.leave(stack(rows))
        got = swap(rows, core)
        yield
        inputs = line.enter([rows, got])
        kernel = functools.partial(backward_kernel, own_rows, wide_labels, n_bits)
        half = own_rows * n_narrow // 2
        keep, send, sums[c] = line.leave(
            tile_call(kernel, me, pattern, at_hi, at_lo, inputs, step, [half, half, 8], 2 * half)
        )
        halves[c] = (keep, send)
        found = []
        yield from halve_stages(line, keep, send, n_dims, found)
        column_grad = line.leave(add_all(found))
        term = lax.dot_general(column_grad, weight[:, cols], (((1,), (1,)), ((), ())), precision=HIGH)
        input_grads[:] = [sum(input_grads, term)]

    def tile_parts():
        own = line.enter(adj_tiles).reshape(block_rows, per_group, size, size)
        tiles.extend(line.leave(prep(own, step)))
        yield

    def feature_rows():
        slots = []
        yield from gather_stages(line, line.enter(features), narrow_dims[::-1], slots, WAVES[2])
        turned.extend(line.leave(turn(slots)))

    def weight_stages(first, last, out):
        while not turned or None in halves[first:last]:
            yield
        there = slot_order(narrow_bits)
        orders = [[there.index(s) for s in slot_order(chunk_bits(c))] for c in range(first, last)]
        parts = [h for c in range(first, last) for h in halves[c]]
        x_hi, x_lo, *parts = line.enter(list(turned) + parts)
        keep, send = line.leave(outer(me, x_hi, x_lo, parts, sum_labels, orders))
        found = []
        yield from halve_stages(line, keep, send, [core] + narrow_dims, found, TAIL)
        total = line.leave(add_all(found, TAIL))
        for dim in z_dims:
            got = swap(total, dim)
            yield
            total, got = line.enter((total, got))
            total = line.leave(add_all([total, got], TAIL))
        parts = []
        yield from gather_stages(line, total, narrow_dims[::-1], parts, False, TAIL)
        parts = line.leave(stack(parts, TAIL))
        got = swap(parts, core)
        yield
        out.extend(line.leave(line.enter([parts, got])))

    def bias_stages(out):
        while None in halves:
            yield
        total = line.leave(jnp.concatenate(sums, axis=1))
        for dim in narrow_dims:
            got = swap(total, dim)
            yield
            total, got = line.enter((total, got))
            total = line.leave(total + got)
        out.append(jnp.sum(total, axis=0) * grad_scale)

    early_parts, weight_parts, bias_out = [], [], []
    lines = {"p": tile_parts()}
    lines.update({str(c): chunk(c) for c in range(count)})
    lines["x"] = feature_rows()
    first = EARLY
    if first:
        lines["v"] = weight_stages(0, first, early_parts)
    lines["w"] = weight_stages(first, count, weight_parts)
    lines["b"] = bias_stages(bias_out)
    for k, name in enumerate("".join(ORDER)):
        with jax.named_scope(f"stage_{name}_{k}"):
            next(lines[name] if name in lines else iter(()), None)
    for stages in lines.values():
        for _ in stages:
            pass
    return (
        jnp.concatenate(outputs, axis=1),
        input_grads[0],
        place(me, early_parts + weight_parts, sum_labels, grad_scale),
        bias_out[0],
    )


def solution(mesh):
    in_specs = (
        P(("wide", "narrow"), None),
        P(),
        P(),
        P("narrow", "wide", None, None, None),
        P("narrow", "wide", None),
        P(("narrow", "wide"), None),
    )
    out_specs = (P(("narrow", "wide"), None), P(("wide", "narrow"), None), P(), P())
    return jax.shard_map(body, mesh=mesh, in_specs=in_specs, out_specs=out_specs, check_vma=False)
```

```python
import functools
import math

import jax
import jax.numpy as jnp
from jax import lax
from jax.experimental import pallas as pl
from jax.experimental.pallas import tpu as pltpu
from jax.sharding import PartitionSpec as P

F32 = jnp.float32
BF16 = jnp.bfloat16
HIGH = lax.Precision.HIGH
WIDTHS = (1, 1, 1, 1)
EARLY = 2
WAVES = (False, False, False)
ORDER = ('01201p32010132x021303x123120131x20302v230v30wvw21wv3wv2wvbwv', '1wbvw3vbw')
SMALL_VMEM = 12 * 1024 * 1024
VMEM_LIMIT = 40 * 1024 * 1024
STAGE = 16000000000.0
TAIL = 0.3


def cost(stages=1.0):
    return pl.CostEstimate(flops=int(STAGE * stages), bytes_accessed=0, transcendentals=0)


def split(x):
    hi = x.astype(BF16)
    return hi, (x - hi.astype(F32)).astype(BF16)


def mm(a, b):
    return jnp.dot(a, b, preferred_element_type=F32)


def bits_of(size):
    return [1 << k for k in range(size.bit_length() - 1)]


def swap(x, dim):
    axis, bit = dim
    size = lax.axis_size(axis)
    return lax.ppermute(x, axis, [(i, i ^ bit) for i in range(size)])


ROWS = 64


def rows_call(fn, out_rows, xs, extra=(), stages=1.0):
    width = xs[0].shape[1]
    outs = [jax.ShapeDtypeStruct((rows, width), F32) for rows in out_rows]
    count, every = len(xs), len(xs) + len(extra)

    def kernel(*refs):
        fn(refs[:count], refs[count:every], refs[every:])

    vmem = pl.BlockSpec(memory_space=pltpu.VMEM)
    return pl.pallas_call(
        kernel,
        in_specs=[vmem] * every,
        out_specs=[vmem] * len(outs),
        out_shape=outs,
        compiler_params=pltpu.CompilerParams(vmem_limit_bytes=SMALL_VMEM),
        cost_estimate=cost(stages),
    )(*xs, *extra)


def blocks_of(rows, step):
    unit = math.gcd(rows, ROWS)

    @pl.loop(0, rows // unit)
    def _(k):
        step(pl.multiple_of(k * unit, unit), unit)


def add_halves(keep, got, stages=1.0):
    half = keep.shape[0] // 2

    def fn(ins, _, outs):
        for k, out in enumerate(outs):

            def step(at, unit, k=k, out=out):
                rows = pl.ds(k * half + at, unit)
                out[pl.ds(at, unit), :] = ins[0][rows, :] + ins[1][rows, :]

            blocks_of(half, step)

    return rows_call(fn, [half, half], [keep, got], stages=stages)


def stack(parts, stages=1.0):
    def fn(ins, _, outs):
        base = 0
        for ref in ins:

            def step(at, unit, base=base, ref=ref):
                outs[0][pl.ds(base + at, unit), :] = ref[pl.ds(at, unit), :]

            blocks_of(ref.shape[0], step)
            base += ref.shape[0]

    return rows_call(fn, [sum(p.shape[0] for p in parts)], parts, stages=stages)[0]


def add_all(terms, stages=1.0):
    def fn(ins, _, outs):
        def step(at, unit):
            rows = pl.ds(at, unit)
            total = ins[0][rows, :]
            for ref in ins[1:]:
                total = total + ref[rows, :]
            outs[0][rows, :] = total

        blocks_of(outs[0].shape[0], step)

    return rows_call(fn, [terms[0].shape[0]], terms, stages=stages)[0]


def activate(keep, got, upstream, bias):
    def fn(ins, extra, outs):
        def step(at, unit):
            rows = pl.ds(at, unit)
            preact = ins[0][rows, :] + ins[1][rows, :] + extra[0][...]
            gate = jax.nn.sigmoid(preact)
            outs[0][rows, :] = preact * gate
            outs[1][rows, :] = ins[2][rows, :] * gate * (1.0 + preact * (1.0 - gate))

        blocks_of(outs[0].shape[0], step)

    rows = keep.shape[0]
    return rows_call(fn, [rows, rows], [keep, got, upstream], [bias.reshape(1, -1)])


class Line:
    def __init__(self):
        self.last = None

    def enter(self, xs):
        if self.last is not None:
            xs, self.last = lax.optimization_barrier((xs, self.last))
        return xs

    def leave(self, xs):
        self.last = xs
        return xs


def gather_stages(line, x, dims, out, waves, stages=1.0):
    parts = [x]
    if waves and len(dims) == 2:
        first, second = swap(x, dims[0]), swap(x, dims[1])
        yield
        last = swap(line.leave(stack([line.enter(first)])), dims[1])
        parts = [x, first, second, last]
    else:
        for dim in dims:
            if len(parts) > 1:
                yield
                parts = line.enter(parts)
                parts = [line.leave(stack(parts, stages))]
            parts = parts + [swap(parts[0], dim)]
    yield
    out.extend(line.enter(parts))


def halve_stages(line, keep, send, dims, out, stages=1.0):
    for k, dim in enumerate(dims):
        got = swap(send, dim)
        yield
        keep, got = line.enter((keep, got))
        if k + 1 == len(dims):
            out.extend((keep, got))
        else:
            keep, send = line.leave(add_halves(keep, got, stages))


def slot_of(owner, me, labels):
    s = owner ^ me
    last = len(labels) - 1
    return sum(((s // label) & 1) << (last - k) for k, label in enumerate(labels))


def slot_order(labels):
    order = [0]
    for label in reversed(labels):
        order = order + [s ^ label for s in order]
    return order


def prep_kernel(tiles_ref, hi_ref, lo_ref, hit_ref, lot_ref):
    steps, per_group, size, _ = tiles_ref.shape
    for r in range(steps):
        for t in range(per_group):
            tile = tiles_ref[r, t]
            hi, lo = split(tile)
            cols = pl.ds(t * size, size)
            hi_ref[r, :, cols] = hi
            lo_ref[r, :, cols] = lo
            hi, lo = split(tile.T)
            hit_ref[r, cols, :] = hi
            lot_ref[r, cols, :] = lo


def prep(tiles, step):
    rows, per_group, size, _ = tiles.shape
    wide = jax.ShapeDtypeStruct((rows, size, per_group * size), BF16)
    tall = jax.ShapeDtypeStruct((rows, per_group * size, size), BF16)
    return pl.pallas_call(
        prep_kernel,
        grid=(rows // step,),
        in_specs=[pl.BlockSpec((step, per_group, size, size), lambda i: (i, 0, 0, 0))],
        out_specs=[pl.BlockSpec((step,) + s.shape[1:], lambda i: (i, 0, 0)) for s in (wide, wide, tall, tall)],
        out_shape=[wide, wide, tall, tall],
        compiler_params=pltpu.CompilerParams(vmem_limit_bytes=VMEM_LIMIT),
        cost_estimate=cost(0),
    )(tiles)


def load_split(refs, hi, lo):
    base = 0
    for ref in refs:
        rows = ref.shape[0]
        hi[pl.ds(base, rows), :], lo[pl.ds(base, rows), :] = split(ref[...])
        base += rows


def block_rows_at(start, size, unit, own_rows, place):
    at = []
    for q in range(size // unit):
        row = start + q * unit
        w = place(row // own_rows) * own_rows + row % own_rows
        at.append(pl.multiple_of(w, unit))
    return at


def products(a_hi, a_lo, b_hi, b_lo):
    return mm(a_hi, b_hi) + (mm(a_hi, b_lo) + mm(a_lo, b_hi))


def gathered(ref, at, unit):
    return jnp.concatenate([ref[pl.ds(w, unit), :] for w in at], axis=0) if len(at) > 1 else ref[pl.ds(at[0], unit), :]


def forward_kernel(own_rows, wide_labels, narrow_labels, me, pattern, a_hi, a_lo, *rest):
    *p_refs, keep, send, p_hi, p_lo, total = rest
    step = pl.program_id(0)
    rows, size, depth = a_hi.shape
    per_group = depth // size
    unit = math.gcd(own_rows, size)

    @pl.when(step == 0)
    def _():
        load_split(p_refs, p_hi, p_lo)

    for i in range(rows):
        r = step * rows + i
        at = []
        for t in range(per_group):
            start = pattern[r * per_group + t] * size
            at += block_rows_at(start, size, unit, own_rows, lambda o: slot_of(o, me[1], narrow_labels))
        acc = products(a_hi[i], a_lo[i], gathered(p_hi, at, unit), gathered(p_lo, at, unit))
        out_at = block_rows_at(r * size, size, unit, own_rows, lambda o: slot_of(o, me[0], wide_labels))
        for q, w in enumerate(out_at):
            total[pl.ds(w, unit), :] = acc[q * unit : (q + 1) * unit]

    @pl.when(step == pl.num_programs(0) - 1)
    def _():
        half = keep.shape[0]
        keep[...] = total[:half]
        send[...] = total[half:]


def tile_call(kernel, me, pattern, a_hi, a_lo, slots, step, outs, total_rows):
    rows = a_hi.shape[0]
    width = slots[0].shape[1]
    in_rows = sum(s.shape[0] for s in slots)
    whole = lambda s: pl.BlockSpec(s, lambda i, *_: (0, 0))
    tile = pl.BlockSpec((step,) + a_hi.shape[1:], lambda i, *_: (i, 0, 0))
    outs = [jax.ShapeDtypeStruct((n, width), F32) for n in outs]
    return pl.pallas_call(
        kernel,
        grid_spec=pltpu.PrefetchScalarGridSpec(
            num_scalar_prefetch=2,
            grid=(rows // step,),
            in_specs=[tile, tile] + [whole(s.shape) for s in slots],
            out_specs=[whole(o.shape) for o in outs],
            scratch_shapes=[
                pltpu.VMEM((in_rows, width), BF16),
                pltpu.VMEM((in_rows, width), BF16),
                pltpu.VMEM((total_rows, width), F32),
            ],
        ),
        out_shape=outs,
        compiler_params=pltpu.CompilerParams(vmem_limit_bytes=VMEM_LIMIT),
        cost_estimate=cost(),
    )(me, pattern, a_hi, a_lo, *slots)


def backward_kernel(own_rows, wide_labels, narrow_labels, me, pattern, a_hi, a_lo, *rest):
    *g_refs, keep, send, sums, g_hi, g_lo, total = rest
    step = pl.program_id(0)
    rows, depth, size = a_hi.shape
    per_group = depth // size
    unit = math.gcd(own_rows, size)

    @pl.when(step == 0)
    def _():
        load_split(g_refs, g_hi, g_lo)
        total[...] = jnp.zeros_like(total)
        sums[...] = sum(jnp.sum(ref[...].reshape(-1, 8, ref.shape[1]), axis=0) for ref in g_refs)

    for i in range(rows):
        r = step * rows + i
        at = block_rows_at(r * size, size, unit, own_rows, lambda o: slot_of(o, me[0], wide_labels))
        acc = products(a_hi[i], a_lo[i], gathered(g_hi, at, unit), gathered(g_lo, at, unit))
        for t in range(per_group):
            start = pattern[r * per_group + t] * size
            out_at = block_rows_at(start, size, unit, own_rows, lambda o: slot_of(o, me[1], narrow_labels))
            for q, w in enumerate(out_at):
                total[pl.ds(w, unit), :] += acc[t * size + q * unit : t * size + (q + 1) * unit]

    @pl.when(step == pl.num_programs(0) - 1)
    def _():
        half = keep.shape[0]
        keep[...] = total[:half]
        send[...] = total[half:]


def turn_kernel(*refs):
    *x_refs, hi, lo = refs
    base = 0
    for ref in x_refs:
        cols = pl.ds(base, ref.shape[0])
        hi[:, cols], lo[:, cols] = split(ref[...].T)
        base += ref.shape[0]


def turn(slots):
    rows = sum(s.shape[0] for s in slots)
    out = jax.ShapeDtypeStruct((slots[0].shape[1], rows), BF16)
    return pl.pallas_call(
        turn_kernel,
        out_shape=[out, out],
        compiler_params=pltpu.CompilerParams(vmem_limit_bytes=VMEM_LIMIT),
        cost_estimate=cost(),
    )(*slots)


def outer_kernel(labels, orders, me, x_hi, x_lo, *rest):
    *s_refs, keep, send, total = rest
    feats, count = x_hi.shape
    pieces = 1 << len(labels)
    unit = feats // pieces
    base = 0
    for k, order in enumerate(orders):
        refs = s_refs[2 * k : 2 * k + 2]
        width = refs[0].shape[1]
        own = count // len(order)
        half = len(order) // 2
        acc = None
        for j, s in enumerate(order):
            cols = pl.ds(s * own, own)
            rows = refs[j // half][pl.ds((j % half) * own, own), :]
            part = products(x_hi[:, cols], x_lo[:, cols], *split(rows))
            acc = part if acc is None else acc + part
        for q in range(pieces):
            w = slot_of(q, me[2], labels) * unit
            total[pl.ds(pl.multiple_of(w, unit), unit), pl.ds(base, width)] = acc[q * unit : (q + 1) * unit]
        base += width
    half = feats // 2
    keep[...] = total[:half]
    send[...] = total[half:]


def outer(me, x_hi, x_lo, parts, labels, orders):
    feats = x_hi.shape[0]
    width = sum(s.shape[1] for s in parts) // 2
    out = jax.ShapeDtypeStruct((feats // 2, width), F32)
    vmem = pl.BlockSpec(memory_space=pltpu.VMEM)
    return pl.pallas_call(
        functools.partial(outer_kernel, labels, orders),
        in_specs=[pl.BlockSpec(memory_space=pltpu.SMEM)] + [vmem] * (2 + len(parts)),
        out_specs=[vmem, vmem],
        out_shape=[out, out],
        scratch_shapes=[pltpu.VMEM((feats, width), F32)],
        compiler_params=pltpu.CompilerParams(vmem_limit_bytes=VMEM_LIMIT),
        cost_estimate=cost(),
    )(me, x_hi, x_lo, *parts)


def place_kernel(scale, labels, me, *refs):
    *p_refs, out = refs
    order = slot_order(labels)
    unit = out.shape[0] // len(order)
    half = len(order) // 2
    base = 0
    for g in range(0, len(p_refs), 2):
        width = p_refs[g].shape[1]
        for k, s in enumerate(order):
            part = p_refs[g + k // half][pl.ds((k % half) * unit, unit), :]
            out[pl.ds(pl.multiple_of((me[2] ^ s) * unit, unit), unit), pl.ds(base, width)] = part * scale
        base += width


def place(me, parts, labels, scale):
    rows = 2 * parts[0].shape[0]
    vmem = pl.BlockSpec(memory_space=pltpu.VMEM)
    return pl.pallas_call(
        functools.partial(place_kernel, scale, labels),
        in_specs=[pl.BlockSpec(memory_space=pltpu.SMEM)] + [vmem] * len(parts),
        out_specs=vmem,
        out_shape=jax.ShapeDtypeStruct((rows, sum(p.shape[1] for p in parts[::2])), F32),
        compiler_params=pltpu.CompilerParams(vmem_limit_bytes=VMEM_LIMIT),
        cost_estimate=cost(),
    )(me, *parts)


def body(features, weight, bias_vec, adj_tiles, pattern, upstream):
    own_rows, feat_width = features.shape
    block_rows, _, per_group, size, _ = adj_tiles.shape
    n_wide, n_narrow = lax.axis_size("wide"), lax.axis_size("narrow")
    me_wide, me_narrow = lax.axis_index("wide"), lax.axis_index("narrow")
    step = math.gcd(block_rows, 6)
    widths = [w * feat_width // sum(WIDTHS) for w in WIDTHS]
    edges = [sum(widths[:c]) for c in range(len(widths) + 1)]
    count = len(widths)
    grad_scale = 1.0 / math.sqrt(own_rows * n_wide * n_narrow)
    line = Line()

    core = ("wide", 1)
    z_bits = bits_of(n_wide)[1:]
    z_dims = [("wide", b) for b in z_bits]
    narrow_bits = bits_of(n_narrow)
    narrow_dims = [("narrow", b) for b in narrow_bits]
    wide_labels = [1] + z_bits
    sum_labels = [1] + [2 * b for b in narrow_bits]
    me = jnp.stack([me_wide, me_narrow, me_wide % 2 + 2 * me_narrow]).astype(jnp.int32)
    pattern = pattern.reshape(-1)

    tiles = []

    outputs, halves, sums = [None] * count, [None] * count, [None] * count
    input_grads, turned = [], []

    def chunk_bits(c):
        return narrow_bits if c % 2 == 0 else narrow_bits[::-1]

    def chunk(c):
        cols = slice(edges[c], edges[c + 1])
        n_bits = chunk_bits(c)
        n_dims = [("narrow", b) for b in n_bits]

        own = line.enter(features)
        own = jnp.dot(own, weight[:, cols], precision=HIGH, preferred_element_type=F32)
        inputs = []
        yield from gather_stages(line, line.leave(own), n_dims[::-1], inputs, WAVES[0])
        while not tiles:
            yield
        a_hi, a_lo, at_hi, at_lo = tiles
        kernel = functools.partial(forward_kernel, own_rows, wide_labels, n_bits)
        half = block_rows * size // 2
        keep, send = line.leave(tile_call(kernel, me, pattern, a_hi, a_lo, inputs, step, [half, half], 2 * half))
        got = swap(send, core)
        yield
        keep, got = line.enter((keep, got))
        keep, send = line.leave(add_halves(keep, got))
        found = []
        yield from halve_stages(line, keep, send, z_dims, found)
        outputs[c], grads = activate(*found, upstream[:, cols], bias_vec[cols])
        line.leave(grads)
        rows = []
        yield from gather_stages(line, grads, z_dims[::-1], rows, WAVES[1])
        rows = line.leave(stack(rows))
        got = swap(rows, core)
        yield
        inputs = line.enter([rows, got])
        kernel = functools.partial(backward_kernel, own_rows, wide_labels, n_bits)
        half = own_rows * n_narrow // 2
        keep, send, sums[c] = line.leave(
            tile_call(kernel, me, pattern, at_hi, at_lo, inputs, step, [half, half, 8], 2 * half)
        )
        halves[c] = (keep, send)
        found = []
        yield from halve_stages(line, keep, send, n_dims, found)
        column_grad = line.leave(add_all(found))
        term = lax.dot_general(column_grad, weight[:, cols], (((1,), (1,)), ((), ())), precision=HIGH)
        input_grads[:] = [sum(input_grads, term)]

    def tile_parts():
        own = line.enter(adj_tiles).reshape(block_rows, per_group, size, size)
        tiles.extend(line.leave(prep(own, step)))
        yield

    def feature_rows():
        slots = []
        yield from gather_stages(line, line.enter(features), narrow_dims[::-1], slots, WAVES[2])
        turned.extend(line.leave(turn(slots)))

    def weight_stages(first, last, out):
        while not turned or None in halves[first:last]:
            yield
        there = slot_order(narrow_bits)
        orders = [[there.index(s) for s in slot_order(chunk_bits(c))] for c in range(first, last)]
        parts = [h for c in range(first, last) for h in halves[c]]
        x_hi, x_lo, *parts = line.enter(list(turned) + parts)
        keep, send = line.leave(outer(me, x_hi, x_lo, parts, sum_labels, orders))
        found = []
        yield from halve_stages(line, keep, send, [core] + narrow_dims, found, TAIL)
        total = line.leave(add_all(found, TAIL))
        for dim in z_dims:
            got = swap(total, dim)
            yield
            total, got = line.enter((total, got))
            total = line.leave(add_all([total, got], TAIL))
        parts = []
        yield from gather_stages(line, total, narrow_dims[::-1], parts, False, TAIL)
        parts = line.leave(stack(parts, TAIL))
        got = swap(parts, core)
        yield
        out.extend(line.leave(line.enter([parts, got])))

    def bias_stages(out):
        while None in halves:
            yield
        total = line.leave(jnp.concatenate(sums, axis=1))
        for dim in narrow_dims:
            got = swap(total, dim)
            yield
            total, got = line.enter((total, got))
            total = line.leave(total + got)
        out.append(jnp.sum(total, axis=0) * grad_scale)

    early_parts, weight_parts, bias_out = [], [], []
    lines = {"p": tile_parts()}
    lines.update({str(c): chunk(c) for c in range(count)})
    lines["x"] = feature_rows()
    first = EARLY
    if first:
        lines["v"] = weight_stages(0, first, early_parts)
    lines["w"] = weight_stages(first, count, weight_parts)
    lines["b"] = bias_stages(bias_out)
    for k, name in enumerate("".join(ORDER)):
        with jax.named_scope(f"stage_{name}_{k}"):
            next(lines[name] if name in lines else iter(()), None)
    for stages in lines.values():
        for _ in stages:
            pass
    return (
        jnp.concatenate(outputs, axis=1),
        input_grads[0],
        place(me, early_parts + weight_parts, sum_labels, grad_scale),
        bias_out[0],
    )


def solution(mesh):
    in_specs = (
        P(("wide", "narrow"), None),
        P(),
        P(),
        P("narrow", "wide", None, None, None),
        P("narrow", "wide", None),
        P(("narrow", "wide"), None),
    )
    out_specs = (P(("narrow", "wide"), None), P(("wide", "narrow"), None), P(), P())
    return jax.shard_map(body, mesh=mesh, in_specs=in_specs, out_specs=out_specs, check_vma=False)
```
